128 devices in a mesh: row: 8 (over z, y_hi), col: 16 (over x, y_lo, core).
Axes of the slice: x: 4, y: 4 (y_hi: 2, y_lo: 2; y = y_hi * 2 + y_lo), z: 4, core: 2. Of those that a mesh axis runs over, the one named last changes fastest.
Arguments:
- amplitudes: bfloat16 [7168, 2048], P('row', 'col'), may hold values from -24 to 24
- integrals: bfloat16 [2048, 61440], P('row', 'col'), may hold values from -0.125 to 0.125
- occ_energy: float32 [7168], P('row'), may hold values from -4 to -1
- slab_energy: float32 [64], P('col'), may hold values from 0.5 to 3
- virt_energy: float32 [960], replicated, may hold values from 0.5 to 3
Outputs:
- amplitude_step: bfloat16 [7168, 61440], P(('row', 'col'))
The draws below stay inside these ranges and needn't reach their ends.
All inputs are finite; a program needn't handle non-finite values.
Results may differ from the reference program's by a relative error of at most 0.001.
Values may be sent and summed in bfloat16 or wider, within the bound.
No kernel may reach another device: no remote copies, remote signals or barrier semaphores. Data moves between devices by JAX's collectives and lax.ppermute only.
A program may use at most 128 MiB of HBM per device.

```python
import jax
import jax.numpy as jnp
from jax import lax

VIRTUALS = 960
A_SLAB = 64
OP_ROW = 896
CD_PAIRS = 2048
OCC_PAIRS = 7168
N_ROW = 8


def levels(stream_key, dims, pieces, least, high):
    def one(position, parts):
        steps = jax.random.uniform(jax.random.fold_in(jax.random.fold_in(stream_key, 6), position), (parts,), jnp.float32, least / len(pieces), high / len(pieces))
        return jnp.repeat(jnp.exp(steps), dims[position] // parts).reshape((-1,) + (1,) * (len(dims) - position - 1))

    level = one(*pieces[0])
    for cut in pieces[1:]:
        level = level * one(*cut)
    return level


def scatter_about(key, shape, deviation, bound, shards=(), dtype=jnp.bfloat16):
    loudness = levels(key, shape, shards, -0.22, 0.18) if shards else 1.0
    values = jax.random.normal(key, shape, jnp.float32) * deviation * loudness
    return jnp.minimum(jnp.maximum(values, -bound), bound).astype(dtype)


def setup_inputs(seed: int = 0) -> dict:
    keys = jax.random.split(jax.random.key(seed), 6)
    amplitudes = scatter_about(keys[0], (OCC_PAIRS, CD_PAIRS), 4.0, 24.0, ((0, 8), (1, 16)))
    integrals = scatter_about(keys[1], (CD_PAIRS, A_SLAB * VIRTUALS), CD_PAIRS ** -0.5, 0.125, ((0, 8), (1, 16)))
    occ_energy = jnp.clip(-4.0 + 3.0 * jax.random.uniform(keys[2], (OCC_PAIRS,), jnp.float32) ** levels(keys[2], (OCC_PAIRS,), ((0, 8),), -0.2, 0.2), -4.0, -1.0)
    slab_energy = jnp.clip(0.5 + 2.5 * jax.random.uniform(keys[3], (A_SLAB,), jnp.float32) ** levels(keys[3], (A_SLAB,), ((0, 16),), -0.2, 0.2), 0.5, 3.0)
    virt_energy = jnp.clip(jax.random.uniform(keys[4], (VIRTUALS,), jnp.float32, 0.5, 3.0), 0.5, 3.0)
    return dict(amplitudes=amplitudes, integrals=integrals, occ_energy=occ_energy, slab_energy=slab_energy, virt_energy=virt_energy)


def reference(amplitudes, integrals, occ_energy, slab_energy, virt_energy):
    virtual_pair = (slab_energy[:, None] + virt_energy[None, :]).reshape(-1)
    row_blocks = amplitudes.reshape(N_ROW, OP_ROW, CD_PAIRS)
    energy_blocks = occ_energy.reshape(N_ROW, OP_ROW)

    def one_block(inputs_pair):
        amp_rows, energies = inputs_pair
        residual = jnp.dot(amp_rows, integrals, preferred_element_type=jnp.float32)
        denominator = energies[:, None] - virtual_pair[None, :]
        return (residual / denominator).astype(jnp.bfloat16)

    result = lax.map(one_block, (row_blocks, energy_blocks))
    return result.reshape(N_ROW * OP_ROW, A_SLAB * VIRTUALS)
```

```python
import functools

import jax
import jax.numpy as jnp
from jax import lax
from jax.experimental import pallas as pl
from jax.experimental.pallas import tpu as pltpu
from jax.sharding import Mesh, PartitionSpec as P

AXES = ("z", "yh", "x", "yl", "c")
SIZES = (4, 2, 4, 2, 2)
Y = ("yh", "yl")
PLANE = ("yh", "x", "yl", "c")
CHUNKS = 3


def shift(value, axis, step, size):
    return lax.ppermute(value, axis, [((i + step) % size, i) for i in range(size)])


def ring(value, axis):
    return jnp.stack([value] + [shift(value, axis, e, 4) for e in (1, 2, 3)])


def product_kernel(p0, q0, p1, q1, own, other, occ_own, occ_other, pair, out):
    yh, x = lax.axis_index("yh"), lax.axis_index("x")
    yl, c = lax.axis_index("yl"), lax.axis_index("c")
    y = yh * 2 + yl
    block, half = pl.program_id(0), pl.program_id(1)
    depth = 128

    def tile(p, q, first_x):
        left, right = [], []
        for d in range(4):
            ex = lax.rem(d - x + 4, 4)
            for f in range(2):
                source = own if f == 0 else other
                low = yh if f == 0 else 1 - yh
                ey = lax.rem(block * 2 + low - y + 4, 4)
                at = (ex, ey) if first_x else (ey, ex)
                left += [p[at], q[at]]
                start = pl.multiple_of(c * depth, depth)
                rest = pl.multiple_of((1 - c) * depth, depth)
                right += [source[d, pl.ds(start, depth), :], source[d, pl.ds(rest, depth), :]]
        a = jnp.concatenate(left, axis=1)
        b = jnp.concatenate(right, axis=0)
        residual = jnp.dot(a, b, preferred_element_type=jnp.float32)
        energy = jnp.where(block == yh, occ_own[half], occ_other[half])
        out[...] = (residual / (energy - pair[...])).astype(out.dtype)

    @pl.when(half == 0)
    def _():
        tile(p0, q0, True)

    @pl.when(half == 1)
    def _():
        tile(p1, q1, False)


def product(panels, own, other, occ_own, occ_other, pair):
    rows = panels[0].shape[2]
    width = own.shape[2]
    whole = pl.BlockSpec(memory_space=pltpu.VMEM)
    return pl.pallas_call(
        product_kernel,
        grid=(2, 2),
        out_shape=jax.ShapeDtypeStruct((4 * rows, width), jnp.bfloat16),
        in_specs=[whole] * 9,
        out_specs=pl.BlockSpec((rows, width), lambda i, h: (i * 2 + h, 0)),
        compiler_params=pltpu.CompilerParams(vmem_limit_bytes=56 << 20),
        cost_estimate=pl.CostEstimate(
            flops=2 * 4 * rows * 2048 * width, bytes_accessed=14 << 20, transcendentals=0
        ),
        name="product",
    )(*panels, own, other, occ_own, occ_other, pair)


def local(amplitudes, integrals, occ_energy, slab_energy, virt_energy):
    yh = lax.axis_index("yh")
    rows = amplitudes.shape[0]
    half = rows // 2
    columns = integrals.shape[1] // 2
    width = columns // CHUNKS

    with jax.named_scope("amplitudes"):
        first = ring(amplitudes[:half], Y)
        second = ring(amplitudes[half:], "x")
        p0 = ring(first, "x")
        p1 = ring(second, Y)
        q0 = shift(p0, "c", 1, 2)
        q1 = shift(p1, "c", 1, 2)
        panels = (p0, q0, p1, q1)
    occ_own = occ_energy.reshape(2, half, 1)
    occ_other = shift(occ_energy, "yh", 1, 2).reshape(2, half, 1)
    pair = (slab_energy[:, None] + virt_energy[None, :]).reshape(2, columns)
    pair = lax.dynamic_index_in_dim(pair, yh, 0, False)

    arrived = []
    for k in range(CHUNKS):
        mine = lax.dynamic_slice(integrals, (0, yh * columns + k * width), (256, width))
        theirs = lax.dynamic_slice(integrals, (0, (1 - yh) * columns + k * width), (256, width))
        own = lax.all_gather(mine, "z", axis=0)
        other = lax.all_gather(shift(theirs, "yh", 1, 2), "z", axis=0)
        part = product(panels, own, other, occ_own, occ_other, pair[None, k * width : (k + 1) * width])
        sent = lax.all_to_all(part.reshape(32, rows // 16, width), PLANE, 0, 0, tiled=True)
        arrived.append(sent.reshape(2, 16, rows // 16, width))
    whole = jnp.stack(arrived)
    return whole.transpose(3, 2, 1, 0, 4).reshape(rows // 16, -1)


def solution(mesh):
    fine = Mesh(mesh.devices.reshape(SIZES), AXES)
    return jax.shard_map(
        local,
        mesh=fine,
        in_specs=(P(("z", "yh"), ("x", "yl", "c")), P(("z", "yh"), ("x", "yl", "c")), P(("z", "yh")), P(("x", "yl", "c")), P()),
        out_specs=P(AXES, None),
        check_vma=False,
    )
```

```python
import jax
import jax.numpy as jnp
from jax import lax
from jax.experimental import pallas as pl
from jax.experimental.pallas import tpu as pltpu
from jax.sharding import Mesh, PartitionSpec as P

AXES = ("z", "yh", "x", "yl", "c")
SIZES = (4, 2, 4, 2, 2)
Y = ("yh", "yl")
PLANE = ("yh", "x", "yl", "c")
WIDTHS = (768, 1152)
DEPTH = 128
ANY = pl.BlockSpec(memory_space=pl.ANY)
VMEM = pl.BlockSpec(memory_space=pltpu.VMEM)


def shift(value, axis, step, size):
    return lax.ppermute(value, axis, [((i + step) % size, i) for i in range(size)])


def ring(value, axis):
    return jnp.stack([value] + [shift(value, axis, e, 4) for e in (1, 2, 3)])


def product_kernel(p0, q0, p1, q1, *refs):
    integrals, (energy, pair, out, panel, block, result, loads, fetches, stores) = refs[:8], refs[8:]
    z, yh, x, yl = (lax.axis_index(a) for a in ("z", "yh", "x", "yl"))
    y = yh * 2 + yl
    rows = p0.shape[2]

    def fetch(d, f):
        slot = pl.multiple_of(lax.rem(z + d, 4) * 512 + f * 256, 256)
        return pltpu.make_async_copy(integrals[d * 2 + f], block.at[pl.ds(slot, 256)], fetches.at[d * 2 + f])

    def load(tile, ex, f, other):
        b, h = tile // 2, tile % 2
        low = yh if f == 0 else 1 - yh
        ey = lax.rem(b * 2 + low - y + 4, 4)
        source = ((p0, q0), (p1, q1))[h][other]
        source = source.at[ex, ey] if h == 0 else source.at[ey, ex]
        slot = pl.multiple_of(lax.rem(x + ex, 4) * 512 + f * 256 + other * DEPTH, DEPTH)
        index = ex * 4 + f * 2 + other
        return pltpu.make_async_copy(source, panel.at[pl.ds(tile * rows, rows), pl.ds(slot, DEPTH)], loads.at[tile, index])

    def store(tile):
        return pltpu.make_async_copy(result.at[tile % 2], out.at[pl.ds(tile * rows, rows)], stores.at[tile % 2])

    pieces = [(ex, f, other) for ex in range(4) for f in range(2) for other in range(2)]
    for d in range(4):
        for f in range(2):
            fetch(d, f).start()
    for tile in range(4):
        for piece in pieces:
            load(tile, *piece).start()
    for d in range(4):
        for f in range(2):
            fetch(d, f).wait()
    for tile in range(4):
        for piece in pieces:
            load(tile, *piece).wait()
        if tile >= 2:
            store(tile - 2).wait()
        residual = jnp.dot(panel[tile * rows : (tile + 1) * rows], block[...], preferred_element_type=jnp.float32)
        denominator = energy[tile * rows : (tile + 1) * rows] - pair[...]
        inverse = pl.reciprocal(denominator, approx=True)
        inverse = inverse * (2.0 - denominator * inverse)
        result[tile % 2] = (residual * inverse).astype(out.dtype)
        store(tile).start()
    store(2).wait()
    store(3).wait()


def product(panels, integrals, energy, pair):
    rows = panels[0].shape[2]
    width = pair.shape[1]
    return pl.pallas_call(
        product_kernel,
        out_shape=jax.ShapeDtypeStruct((4 * rows, width), jnp.bfloat16),
        in_specs=[ANY] * 12 + [VMEM] * 2,
        out_specs=ANY,
        scratch_shapes=[
            pltpu.VMEM((4 * rows, 2048), jnp.bfloat16),
            pltpu.VMEM((2048, width), jnp.bfloat16),
            pltpu.VMEM((2, rows, width), jnp.bfloat16),
            pltpu.SemaphoreType.DMA((4, 16)),
            pltpu.SemaphoreType.DMA((8,)),
            pltpu.SemaphoreType.DMA((2,)),
        ],
        compiler_params=pltpu.CompilerParams(vmem_limit_bytes=40 << 20),
        cost_estimate=pl.CostEstimate(
            flops=2 * 4 * rows * 2048 * width, bytes_accessed=14 << 20, transcendentals=0
        ),
        name="product",
    )(*panels, *integrals, energy, pair)


def place_kernel(offset, columns, piece, *refs):
    out, sems = refs[-2:]
    width = piece.shape[3]

    def copy(h, s):
        at = s * 2 * columns + h * columns + offset
        return pltpu.make_async_copy(piece.at[h, s], out.at[:, pl.ds(at, width)], sems.at[h, s])

    for s in range(16):
        for h in range(2):
            copy(h, s).start()
    for s in range(16):
        for h in range(2):
            copy(h, s).wait()


def place(piece, offset, columns, whole):
    rows = piece.shape[2]
    operands = [piece] if whole is None else [piece, whole]
    return pl.pallas_call(
        lambda *refs: place_kernel(offset, columns, *refs),
        out_shape=jax.ShapeDtypeStruct((rows, 32 * columns), jnp.bfloat16),
        in_specs=[ANY] * len(operands),
        out_specs=ANY,
        scratch_shapes=[pltpu.SemaphoreType.DMA((2, 16))],
        input_output_aliases={} if whole is None else {1: 0},
        cost_estimate=pl.CostEstimate(flops=0, bytes_accessed=4 * piece.size, transcendentals=0),
        name="place",
    )(*operands)


def local(amplitudes, integrals, occ_energy, slab_energy, virt_energy):
    yh, c = lax.axis_index("yh"), lax.axis_index("c")
    rows = amplitudes.shape[0]
    half = rows // 2
    columns = integrals.shape[1] // 2

    with jax.named_scope("amplitudes"):
        first = ring(amplitudes[:half], Y)
        second = ring(amplitudes[half:], "x")
        p0 = ring(first, "x")
        p1 = ring(second, Y)
        q0 = shift(p0, "c", 1, 2)
        q1 = shift(p1, "c", 1, 2)
        panels = (p0, q0, p1, q1)
    energies = jnp.stack([occ_energy, shift(occ_energy, "yh", 1, 2)])
    energy = jnp.concatenate([energies[yh], energies[1 - yh]]).reshape(2 * rows, 1)
    pair = (slab_energy[:, None] + virt_energy[None, :]).reshape(2, columns)
    pair = lax.dynamic_index_in_dim(pair, yh, 0, True)

    def part(h, offset, width):
        at = h * columns + offset
        return jnp.concatenate(
            [lax.dynamic_slice(integrals, (o * DEPTH, at), (DEPTH, width)) for o in (c, 1 - c)]
        )

    whole, offset = None, 0
    for width in WIDTHS:
        own = part(yh, offset, width)
        other = shift(part(1 - yh, offset, width), "yh", 1, 2)
        pieces = [own, other]
        for d in (1, 2, 3):
            pieces += [shift(own, "z", d, 4), shift(other, "z", d, 4)]
        update = product(panels, pieces, energy, pair[:, offset : offset + width])
        sent = lax.all_to_all(update.reshape(32, rows // 16, width), PLANE, 0, 0, tiled=True)
        whole = place(sent.reshape(2, 16, rows // 16, width), offset, columns, whole)
        offset += width
    return whole


def solution(mesh):
    fine = Mesh(mesh.devices.reshape(SIZES), AXES)
    split = P(("z", "yh"), ("x", "yl", "c"))
    return jax.shard_map(
        local,
        mesh=fine,
        in_specs=(split, split, P(("z", "yh")), P(("x", "yl", "c")), P()),
        out_specs=P(AXES, None),
        check_vma=False,
    )
```

```python
import functools

import jax
import jax.numpy as jnp
from jax import lax
from jax.experimental import pallas as pl
from jax.experimental.pallas import tpu as pltpu
from jax.sharding import Mesh, PartitionSpec as P

AXES = ("z", "yh", "x", "yl", "c")
SIZES = (4, 2, 4, 2, 2)
PLANE = ("yh", "x", "yl")
CHIPS = 16
PAIRS = 256
DEPTH = 128
CUT = 1024
STEPS = (0, 1, 3, 2)
Y = ("yh", "yl")
HBM = pl.BlockSpec(memory_space=pltpu.HBM)
VMEM = pl.BlockSpec(memory_space=pltpu.VMEM)
HINT = pl.CostEstimate(flops=10**6, bytes_accessed=1 << 16, transcendentals=0)


def shift(value, axis, step, size):
    return lax.ppermute(value, axis, [((i + step) % size, i) for i in range(size)])


def around(value, axis):
    return tuple(shift(value, axis, step, 4) for step in STEPS[1:])


def product_kernel(held, at_column, *refs):
    panels, refs = refs[:4], refs[4:]
    arrays, energy, pair = refs[:held], refs[held], refs[held + 1]
    out, panel, block, result, loads, fetches, stores = refs[-7:]
    z, yh, yl = lax.axis_index("z"), lax.axis_index("yh"), lax.axis_index("yl")
    rows, width = panels[0].shape[1], pair.shape[1]
    cuts = [(at, min(CUT, width - at)) for at in range(0, width, CUT)]

    def load(i, x):
        there = lax.rem(yh * 2 + yl + STEPS[i], 4)
        row = pl.multiple_of(there // 2 * rows, rows)
        slot = pl.multiple_of((x * 2 + lax.rem(there, 2)) * PAIRS, PAIRS)
        return pltpu.make_async_copy(
            panels[i].at[x], panel.at[pl.ds(row, rows), pl.ds(slot, PAIRS)], loads.at[i, x]
        )

    def fetch(cut):
        at, size = cuts[cut]
        copies = []
        for i in range(8):
            if i < 4:
                low, source = yh, arrays[0].at[i]
            else:
                low, source = 1 - yh, arrays[i - 3]
            slot = pl.multiple_of(lax.rem(z + STEPS[i % 4], 4) * 2 * PAIRS + low * PAIRS, PAIRS)
            target = block.at[pl.ds(slot, PAIRS), pl.ds(at, size)]
            sem = fetches.at[cut, len(copies)]
            copies.append(pltpu.make_async_copy(source.at[:, pl.ds(at, size)], target, sem))
        return copies

    def store(b):
        here = pl.ds(b * rows, rows)
        return pltpu.make_async_copy(result.at[here], out.at[here, pl.ds(at_column, width)], stores.at[b])

    copies = [load(i, x) for i in range(4) for x in range(4)]
    pieces = [fetch(cut) for cut in range(len(cuts))]
    for copy in copies + [copy for piece in pieces for copy in piece]:
        copy.start()
    for copy in copies:
        copy.wait()
    for cut, (at, size) in enumerate(cuts):
        for copy in pieces[cut]:
            copy.wait()
        for b in range(2):
            here = (pl.ds(b * rows, rows), pl.ds(at, size))
            residual = jnp.dot(panel[here[0], :], block[:, here[1]], preferred_element_type=jnp.float32)
            denominator = energy[here[0]] - pair[:, here[1]]
            inverse = pl.reciprocal(denominator, approx=True)
            inverse = inverse * (2.0 - denominator * inverse)
            result[here] = (residual * inverse).astype(out.dtype)
            if cut == len(cuts) - 1:
                store(b).start()
    for b in range(2):
        store(b).wait()


def product(panels, arrays, energy, pair, started=None):
    rows, width = energy.shape[0], pair.shape[1]
    cuts = -(-width // CUT)
    operands = [*panels, *arrays, energy, pair] + ([] if started is None else [started])
    at_column = 0 if started is None else width
    return pl.pallas_call(
        functools.partial(product_kernel, len(arrays), at_column),
        out_shape=jax.ShapeDtypeStruct((rows, 2 * width), jnp.bfloat16),
        in_specs=[HBM] * (4 + len(arrays)) + [VMEM] * 2 + ([] if started is None else [HBM]),
        out_specs=HBM,
        scratch_shapes=[
            pltpu.VMEM((rows, 8 * PAIRS), jnp.bfloat16),
            pltpu.VMEM((8 * PAIRS, width), jnp.bfloat16),
            pltpu.VMEM((rows, width), jnp.bfloat16),
            pltpu.SemaphoreType.DMA((4, 4)),
            pltpu.SemaphoreType.DMA((cuts, 8)),
            pltpu.SemaphoreType.DMA((2,)),
        ],
        input_output_aliases={} if started is None else {len(operands) - 1: 0},
        compiler_params=pltpu.CompilerParams(vmem_limit_bytes=60 << 20),
        cost_estimate=HINT,
        name="product",
    )(*operands)


def place_kernel(columns, piece, out, stage, loads, stores):
    c = lax.axis_index("c")

    def load(s):
        return pltpu.make_async_copy(piece.at[s], stage.at[s], loads.at[s])

    def store(s, h):
        at = (s % 8) * 4 * columns + s // 8 * columns + (1 - c if h else c) * 2 * columns
        target = out.at[:, pl.ds(pl.multiple_of(at, DEPTH), columns)]
        return pltpu.make_async_copy(stage.at[s, :, pl.ds(h * columns, columns)], target, stores.at[s, h])

    for s in range(CHIPS):
        load(s).start()
    for s in range(CHIPS):
        load(s).wait()
        for h in range(2):
            store(s, h).start()
    for s in range(CHIPS):
        for h in range(2):
            store(s, h).wait()


def place(piece):
    rows, width = piece.shape[1:]
    return pl.pallas_call(
        functools.partial(place_kernel, width // 2),
        out_shape=jax.ShapeDtypeStruct((rows, CHIPS * width), jnp.bfloat16),
        in_specs=[HBM],
        out_specs=HBM,
        scratch_shapes=[
            pltpu.VMEM(piece.shape, jnp.bfloat16),
            pltpu.SemaphoreType.DMA((CHIPS,)),
            pltpu.SemaphoreType.DMA((CHIPS, 2)),
        ],
        compiler_params=pltpu.CompilerParams(vmem_limit_bytes=60 << 20),
        cost_estimate=HINT,
        name="place",
    )(piece)


def local(amplitudes, integrals, occ_energy, slab_energy, virt_energy):
    yh, c = lax.axis_index("yh"), lax.axis_index("c")
    portion = amplitudes.shape[0] // CHIPS
    columns = integrals.shape[1] // 2
    after = lax.optimization_barrier

    def pick(value, index, axis):
        return lax.dynamic_index_in_dim(value, index, axis, False)

    def part(h):
        return lax.dynamic_slice(integrals, (0, h * columns), (PAIRS, columns))

    def swap(value):
        return shift(value, "c", 1, 2)

    mine, away = part(yh), part(1 - yh)
    up, down = around(mine, "z")[:2]
    other = shift(away, "yh", 1, 2)
    rows = amplitudes.reshape(8, 2, portion, -1)
    kept = pick(rows, c, 1).reshape(8 * portion, -1)
    got = swap(pick(rows, 1 - c, 1).reshape(8 * portion, -1))
    both = jnp.where(c == 0, jnp.concatenate([kept, got], 1), jnp.concatenate([got, kept], 1))
    occ = pick(occ_energy.reshape(8, 2, portion), c, 1).reshape(1, -1)
    along = lax.all_gather(both, "x", axis=0)

    other, along, occ, slab_energy = after((other, along, occ, slab_energy))
    others = around(other, "z")
    two = shift(up[:DEPTH], "z", 1, 4), shift(down[DEPTH:], "z", 3, 4)
    panels = (along,) + around(along, Y)
    occ_other = shift(occ, "yh", 1, 2)
    slab_other = swap(slab_energy)
    here = jnp.stack([mine, up, down, jnp.concatenate(two)])
    energy = jnp.where(yh == 0, jnp.concatenate([occ, occ_other]), jnp.concatenate([occ_other, occ]))
    energy = energy.reshape(-1, 1)

    def pair(slab):
        pairs = (slab[:, None] + virt_energy[None, :]).reshape(2, columns)
        return pick(pairs, yh, 0).reshape(1, -1)

    pairs, pairs2 = pair(slab_energy), pair(slab_other)
    others, here, panels, energy, pairs, pairs2 = after((others, here, panels, energy, pairs, pairs2))
    there = tuple(swap(value) for value in (here, other) + others)
    update = product(panels, (here, other) + others, energy, pairs)
    update = product(panels, there, energy, pairs2, update)
    return place(lax.all_to_all(update.reshape(CHIPS, portion, -1), PLANE, 0, 0, tiled=True))


def solution(mesh):
    fine = Mesh(mesh.devices.reshape(SIZES), AXES)
    split = P(("z", "yh"), ("x", "yl", "c"))
    return jax.shard_map(
        local,
        mesh=fine,
        in_specs=(split, split, P(("z", "yh")), P(("x", "yl", "c")), P()),
        out_specs=P(AXES, None),
        check_vma=False,
    )
```

```python
import functools

import jax
import jax.numpy as jnp
from jax import lax
from jax.experimental import pallas as pl
from jax.experimental.pallas import tpu as pltpu
from jax.sharding import Mesh, PartitionSpec as P

AXES = ("z", "yh", "x", "yl", "c")
SIZES = (4, 2, 4, 2, 2)
PLANE = ("yh", "x", "yl")
CHIPS = 16
PAIRS = 256
DEPTH = 128
CUTS = ((0, 256), (256, 640), (896, 1024))
STEPS = (0, 1, 3, 2)
Y = ("yh", "yl")
HBM = pl.BlockSpec(memory_space=pltpu.HBM)
VMEM = pl.BlockSpec(memory_space=pltpu.VMEM)
HINT = pl.CostEstimate(flops=10**6, bytes_accessed=1 << 16, transcendentals=0)


def shift(value, axis, step, size):
    return lax.ppermute(value, axis, [((i + step) % size, i) for i in range(size)])


def near(value, axis):
    return shift(value, axis, 1, 4), shift(value, axis, 3, 4)


def far(up, down, axis):
    cut = up.shape[0] // 2
    return shift(up[:cut], axis, 1, 4), shift(down[cut:], axis, 3, 4)


def product_kernel(at_column, *refs):
    panels, arrays, energy, pair = refs[:5], refs[5:11], refs[11], refs[12]
    out, panel, block, result, loads, fetches, stores = refs[-7:]
    z, yh, yl = lax.axis_index("z"), lax.axis_index("yh"), lax.axis_index("yl")
    rows, width = panels[0].shape[1], pair.shape[1]
    cuts = [(at, size) for at, size in CUTS if at < width]

    def load(i, x):
        there = lax.rem(yh * 2 + yl + STEPS[i], 4)
        row = pl.multiple_of(there // 2 * rows, rows)
        slot = pl.multiple_of((x * 2 + lax.rem(there, 2)) * PAIRS, PAIRS)
        source = panels[i].at[x] if i < 3 else panels[3 + x // 2].at[x % 2]
        return pltpu.make_async_copy(source, panel.at[pl.ds(row, rows), pl.ds(slot, PAIRS)], loads.at[i, x])

    def fetch(cut):
        at, size = cuts[cut]
        copies = []
        parts = [(yh, STEPS[i], 0, arrays[0].at[i]) for i in range(4)]
        parts += [(1 - yh, STEPS[i], 0, arrays[i + 1]) for i in range(3)]
        parts += [(1 - yh, 2, i * DEPTH, arrays[i + 4]) for i in range(2)]
        for low, step, skip, source in parts:
            count = source.shape[0]
            slot = pl.multiple_of(lax.rem(z + step, 4) * 2 * PAIRS + low * PAIRS + skip, DEPTH)
            target = block.at[pl.ds(slot, count), pl.ds(at, size)]
            sem = fetches.at[cut, len(copies)]
            copies.append(pltpu.make_async_copy(source.at[:, pl.ds(at, size)], target, sem))
        return copies

    def store(cut, b):
        at, size = cuts[cut]
        here = pl.ds(b * rows, rows)
        source = result.at[here, pl.ds(at, size)]
        return pltpu.make_async_copy(source, out.at[here, pl.ds(at_column + at, size)], stores.at[cut, b])

    copies = [load(i, x) for i in range(4) for x in range(4)]
    pieces = [fetch(cut) for cut in range(len(cuts))]
    for copy in copies + [copy for piece in pieces for copy in piece]:
        copy.start()
    for copy in copies:
        copy.wait()
    for cut, (at, size) in enumerate(cuts):
        for copy in pieces[cut]:
            copy.wait()
        for b in range(2):
            here = (pl.ds(b * rows, rows), pl.ds(at, size))
            residual = jnp.dot(panel[here[0], :], block[:, here[1]], preferred_element_type=jnp.float32)
            denominator = energy[here[0]] - pair[:, here[1]]
            inverse = pl.reciprocal(denominator, approx=True)
            inverse = inverse * (2.0 - denominator * inverse)
            result[here] = (residual * inverse).astype(out.dtype)
            store(cut, b).start()
    for cut in range(len(cuts)):
        for b in range(2):
            store(cut, b).wait()


def product(panels, arrays, energy, pair, started=None):
    rows, width = energy.shape[0], pair.shape[1]
    cuts = len(CUTS)
    operands = [*panels, *arrays, energy, pair] + ([] if started is None else [started])
    at_column = 0 if started is None else width
    return pl.pallas_call(
        functools.partial(product_kernel, at_column),
        out_shape=jax.ShapeDtypeStruct((rows, 2 * width), jnp.bfloat16),
        in_specs=[HBM] * (len(panels) + len(arrays)) + [VMEM] * 2 + ([] if started is None else [HBM]),
        out_specs=HBM,
        scratch_shapes=[
            pltpu.VMEM((rows, 8 * PAIRS), jnp.bfloat16),
            pltpu.VMEM((8 * PAIRS, width), jnp.bfloat16),
            pltpu.VMEM((rows, width), jnp.bfloat16),
            pltpu.SemaphoreType.DMA((4, 4)),
            pltpu.SemaphoreType.DMA((cuts, 9)),
            pltpu.SemaphoreType.DMA((cuts, 2)),
        ],
        input_output_aliases={} if started is None else {len(operands) - 1: 0},
        compiler_params=pltpu.CompilerParams(vmem_limit_bytes=60 << 20),
        cost_estimate=HINT,
        name="product",
    )(*operands)


def place_kernel(columns, piece, out, stores):
    c = lax.axis_index("c")
    copies = []
    for s in range(CHIPS):
        for h in range(2):
            at = (s % 8) * 4 * columns + s // 8 * columns + (1 - c if h else c) * 2 * columns
            target = out.at[:, pl.ds(pl.multiple_of(at, DEPTH), columns)]
            source = piece.at[s, :, pl.ds(h * columns, columns)]
            copies.append(pltpu.make_async_copy(source, target, stores.at[s, h]))
    for copy in copies:
        copy.start()
    for copy in copies:
        copy.wait()


def place(piece):
    rows, width = piece.shape[1:]
    return pl.pallas_call(
        functools.partial(place_kernel, width // 2),
        out_shape=jax.ShapeDtypeStruct((rows, CHIPS * width), jnp.bfloat16),
        in_specs=[VMEM],
        out_specs=HBM,
        scratch_shapes=[pltpu.SemaphoreType.DMA((CHIPS, 2))],
        compiler_params=pltpu.CompilerParams(vmem_limit_bytes=16 << 20),
        cost_estimate=HINT,
        name="place",
    )(piece)


def local(amplitudes, integrals, occ_energy, slab_energy, virt_energy):
    yh, c = lax.axis_index("yh"), lax.axis_index("c")
    portion = amplitudes.shape[0] // CHIPS
    columns = integrals.shape[1] // 2
    after = lax.optimization_barrier

    def pick(value, index, axis):
        return lax.dynamic_index_in_dim(value, index, axis, False)

    def part(h):
        return lax.dynamic_slice(integrals, (0, h * columns), (PAIRS, columns))

    def swap(value):
        return shift(value, "c", 1, 2)

    mine, away = part(yh), part(1 - yh)
    up, down = near(mine, "z")
    other = shift(away, "yh", 1, 2)
    rows = amplitudes.reshape(8, 2, portion, -1)
    kept = pick(rows, c, 1).reshape(8 * portion, -1)
    got = swap(pick(rows, 1 - c, 1).reshape(8 * portion, -1))
    both = jnp.where(c == 0, jnp.concatenate([kept, got], 1), jnp.concatenate([got, kept], 1))
    occ = pick(occ_energy.reshape(8, 2, portion), c, 1).reshape(1, -1)
    along = lax.all_gather(both, "x", axis=0)

    other, along, up, down, occ, slab_energy = after((other, along, up, down, occ, slab_energy))
    others = near(other, "z")
    panels = near(along, Y)
    two = far(up, down, "z")
    here = jnp.stack([mine, up, down, jnp.concatenate(two)])
    others, panels, here, slab_energy, occ = after((others, panels, here, slab_energy, occ))
    occ_other = shift(occ, "yh", 1, 2)
    other2, slab_other = swap(other), swap(slab_energy)
    others = others + far(*others, "z")
    panels = (along,) + panels + far(*panels, Y)
    energy = jnp.where(yh == 0, jnp.concatenate([occ, occ_other]), jnp.concatenate([occ_other, occ]))
    energy = energy.reshape(-1, 1)

    def pair(slab):
        pairs = (slab[:, None] + virt_energy[None, :]).reshape(2, columns)
        return pick(pairs, yh, 0).reshape(1, -1)

    pairs, pairs2 = pair(slab_energy), pair(slab_other)
    others, here, panels, energy, pairs, pairs2, other2 = after(
        (others, here, panels, energy, pairs, pairs2, other2)
    )
    there = (swap(here), other2) + tuple(swap(value) for value in others)
    update = product(panels, (here, other) + others, energy, pairs)
    update = product(panels, there, energy, pairs2, update)
    return place(lax.all_to_all(update.reshape(CHIPS, portion, -1), PLANE, 0, 0, tiled=True))


def solution(mesh):
    fine = Mesh(mesh.devices.reshape(SIZES), AXES)
    split = P(("z", "yh"), ("x", "yl", "c"))
    return jax.shard_map(
        local,
        mesh=fine,
        in_specs=(split, split, P(("z", "yh")), P(("x", "yl", "c")), P()),
        out_specs=P(AXES, None),
        check_vma=False,
    )
```

```python
import functools

import jax
import jax.numpy as jnp
from jax import lax
from jax.experimental import pallas as pl
from jax.experimental.pallas import tpu as pltpu
from jax.sharding import Mesh, PartitionSpec as P

AXES = ("z", "yh", "x", "yl", "c")
SIZES = (4, 2, 4, 2, 2)
PLANE = ("yh", "x", "yl")
CHIPS = 16
PAIRS = 256
DEPTH = 128
CUTS = ((0, 256), (256, 640), (896, 1024))
STEPS = (0, 1, 3, 2)
Y = ("yh", "yl")
HBM = pl.BlockSpec(memory_space=pltpu.HBM)
VMEM = pl.BlockSpec(memory_space=pltpu.VMEM)
HINT = pl.CostEstimate(flops=10**6, bytes_accessed=1 << 16, transcendentals=0)


def shift(value, axis, step, size):
    return lax.ppermute(value, axis, [((i + step) % size, i) for i in range(size)])


def near(value, axis):
    return shift(value, axis, 1, 4), shift(value, axis, 3, 4)


def far(up, down, axis):
    cut = up.shape[0] // 2
    return shift(up[:cut], axis, 1, 4), shift(down[cut:], axis, 3, 4)


def product_kernel(at_column, *refs):
    panels, arrays, energy, pair = refs[:5], refs[5:11], refs[11], refs[12]
    out, panel, block, result, loads, fetches, stores = refs[-7:]
    z, yh, yl = lax.axis_index("z"), lax.axis_index("yh"), lax.axis_index("yl")
    rows, width = panels[0].shape[1], pair.shape[1]
    cuts = [(at, size) for at, size in CUTS if at < width]

    def load(i, x):
        there = lax.rem(yh * 2 + yl + STEPS[i], 4)
        row = pl.multiple_of(there // 2 * rows, rows)
        slot = pl.multiple_of((x * 2 + lax.rem(there, 2)) * PAIRS, PAIRS)
        source = panels[i].at[x] if i < 3 else panels[3 + x // 2].at[x % 2]
        return pltpu.make_async_copy(source, panel.at[pl.ds(row, rows), pl.ds(slot, PAIRS)], loads.at[i, x])

    def fetch(cut):
        at, size = cuts[cut]
        copies = []
        parts = [(yh, STEPS[i], 0, arrays[0].at[i]) for i in range(4)]
        parts += [(1 - yh, STEPS[i], 0, arrays[i + 1]) for i in range(3)]
        parts += [(1 - yh, 2, i * DEPTH, arrays[i + 4]) for i in range(2)]
        for low, step, skip, source in parts:
            count = source.shape[0]
            slot = pl.multiple_of(lax.rem(z + step, 4) * 2 * PAIRS + low * PAIRS + skip, DEPTH)
            target = block.at[pl.ds(slot, count), pl.ds(at, size)]
            sem = fetches.at[cut, len(copies)]
            copies.append(pltpu.make_async_copy(source.at[:, pl.ds(at, size)], target, sem))
        return copies

    def store(cut, b):
        at, size = cuts[cut]
        here = pl.ds(b * rows, rows)
        source = result.at[here, pl.ds(at, size)]
        return pltpu.make_async_copy(source, out.at[here, pl.ds(at_column + at, size)], stores.at[cut, b])

    copies = [load(i, x) for i in range(4) for x in range(4)]
    pieces = [fetch(cut) for cut in range(len(cuts))]
    for copy in copies + [copy for piece in pieces for copy in piece]:
        copy.start()
    for copy in copies:
        copy.wait()
    for cut, (at, size) in enumerate(cuts):
        for copy in pieces[cut]:
            copy.wait()
        for b in range(2):
            here = (pl.ds(b * rows, rows), pl.ds(at, size))
            residual = jnp.dot(panel[here[0], :], block[:, here[1]], preferred_element_type=jnp.float32)
            denominator = energy[here[0]] - pair[:, here[1]]
            inverse = pl.reciprocal(denominator, approx=True)
            inverse = inverse * (2.0 - denominator * inverse)
            result[here] = (residual * inverse).astype(out.dtype)
            store(cut, b).start()
    for cut in range(len(cuts)):
        for b in range(2):
            store(cut, b).wait()


def product(panels, arrays, energy, pair, started=None):
    rows, width = energy.shape[0], pair.shape[1]
    cuts = len(CUTS)
    operands = [*panels, *arrays, energy, pair] + ([] if started is None else [started])
    at_column = 0 if started is None else width
    return pl.pallas_call(
        functools.partial(product_kernel, at_column),
        out_shape=jax.ShapeDtypeStruct((rows, 2 * width), jnp.bfloat16),
        in_specs=[HBM] * (len(panels) + len(arrays)) + [VMEM] * 2 + ([] if started is None else [HBM]),
        out_specs=HBM,
        scratch_shapes=[
            pltpu.VMEM((rows, 8 * PAIRS), jnp.bfloat16),
            pltpu.VMEM((8 * PAIRS, width), jnp.bfloat16),
            pltpu.VMEM((rows, width), jnp.bfloat16),
            pltpu.SemaphoreType.DMA((4, 4)),
            pltpu.SemaphoreType.DMA((cuts, 9)),
            pltpu.SemaphoreType.DMA((cuts, 2)),
        ],
        input_output_aliases={} if started is None else {len(operands) - 1: 0},
        compiler_params=pltpu.CompilerParams(vmem_limit_bytes=60 << 20),
        cost_estimate=HINT,
        name="product",
    )(*operands)


def place_kernel(columns, piece, out, stores):
    c = lax.axis_index("c")
    copies = []
    for s in range(CHIPS):
        for h in range(2):
            at = (s % 8) * 4 * columns + s // 8 * columns + (1 - c if h else c) * 2 * columns
            target = out.at[:, pl.ds(pl.multiple_of(at, DEPTH), columns)]
            source = piece.at[s, :, pl.ds(h * columns, columns)]
            copies.append(pltpu.make_async_copy(source, target, stores.at[s, h]))
    for copy in copies:
        copy.start()
    for copy in copies:
        copy.wait()


def place(piece):
    rows, width = piece.shape[1:]
    return pl.pallas_call(
        functools.partial(place_kernel, width // 2),
        out_shape=jax.ShapeDtypeStruct((rows, CHIPS * width), jnp.bfloat16),
        in_specs=[VMEM],
        out_specs=HBM,
        scratch_shapes=[pltpu.SemaphoreType.DMA((CHIPS, 2))],
        compiler_params=pltpu.CompilerParams(vmem_limit_bytes=16 << 20),
        cost_estimate=HINT,
        name="place",
    )(piece)


def local(amplitudes, integrals, occ_energy, slab_energy, virt_energy):
    yh, c = lax.axis_index("yh"), lax.axis_index("c")
    portion = amplitudes.shape[0] // CHIPS
    columns = integrals.shape[1] // 2
    after = lax.optimization_barrier

    def pick(value, index, axis):
        return lax.dynamic_index_in_dim(value, index, axis, False)

    def part(h):
        return lax.dynamic_slice(integrals, (0, h * columns), (PAIRS, columns))

    def swap(value):
        return shift(value, "c", 1, 2)

    mine, away = part(yh), part(1 - yh)
    up, down = near(mine, "z")
    other = shift(away, "yh", 1, 2)
    rows = amplitudes.reshape(8, 2, portion, -1)
    kept = pick(rows, c, 1).reshape(8 * portion, -1)
    got = swap(pick(rows, 1 - c, 1).reshape(8 * portion, -1))
    both = jnp.where(c == 0, jnp.concatenate([kept, got], 1), jnp.concatenate([got, kept], 1))
    occ = pick(occ_energy.reshape(8, 2, portion), c, 1).reshape(1, -1)
    along = lax.all_gather(both, "x", axis=0)

    other, along, up, down, occ, slab_energy = after((other, along, up, down, occ, slab_energy))
    others = near(other, "z")
    panels = near(along, Y)
    two = far(up, down, "z")
    here = jnp.stack([mine, up, down, jnp.concatenate(two)])
    panels, slab_energy, occ = after((panels, slab_energy, occ))
    occ_other = shift(occ, "yh", 1, 2)
    other2, slab_other = swap(other), swap(slab_energy)
    others = others + far(*others, "z")
    panels = (along,) + panels + far(*panels, Y)
    energy = jnp.where(yh == 0, jnp.concatenate([occ, occ_other]), jnp.concatenate([occ_other, occ]))
    energy = energy.reshape(-1, 1)

    def pair(slab):
        pairs = (slab[:, None] + virt_energy[None, :]).reshape(2, columns)
        return pick(pairs, yh, 0).reshape(1, -1)

    pairs, pairs2 = pair(slab_energy), pair(slab_other)
    others, here, panels, energy, pairs, pairs2, other2 = after(
        (others, here, panels, energy, pairs, pairs2, other2)
    )
    there = (swap(here), other2) + tuple(swap(value) for value in others)
    update = product(panels, (here, other) + others, energy, pairs)
    update = product(panels, there, energy, pairs2, update)
    return place(lax.all_to_all(update.reshape(CHIPS, portion, -1), PLANE, 0, 0, tiled=True))


def solution(mesh):
    fine = Mesh(mesh.devices.reshape(SIZES), AXES)
    split = P(("z", "yh"), ("x", "yl", "c"))
    return jax.shard_map(
        local,
        mesh=fine,
        in_specs=(split, split, P(("z", "yh")), P(("x", "yl", "c")), P()),
        out_specs=P(AXES, None),
        check_vma=False,
    )
```

```python
import functools

import jax
import jax.numpy as jnp
from jax import lax
from jax.experimental import pallas as pl
from jax.experimental.pallas import tpu as pltpu
from jax.sharding import Mesh, PartitionSpec as P

AXES = ("z", "yh", "x", "yl", "c")
SIZES = (4, 2, 4, 2, 2)
PLANE = ("yh", "x", "yl")
CHIPS = 16
PAIRS = 256
DEPTH = 128
CUTS = ((0, 256), (256, 640), (896, 1024))
STEPS = (0, 1, 3, 2)
Y = ("yh", "yl")
HBM = pl.BlockSpec(memory_space=pltpu.HBM)
VMEM = pl.BlockSpec(memory_space=pltpu.VMEM)
HINT = pl.CostEstimate(flops=10**6, bytes_accessed=1 << 16, transcendentals=0)


def shift(value, axis, step, size):
    return lax.ppermute(value, axis, [((i + step) % size, i) for i in range(size)])


def near(value, axis):
    return shift(value, axis, 1, 4), shift(value, axis, 3, 4)


def far(up, down, axis):
    cut = up.shape[0] // 2
    return shift(up[:cut], axis, 1, 4), shift(down[cut:], axis, 3, 4)


def product_kernel(at_column, *refs):
    panels, arrays, energy, pair = refs[:5], refs[5:11], refs[11], refs[12]
    out, panel, block, result, loads, fetches, stores = refs[-7:]
    z, yh, yl = lax.axis_index("z"), lax.axis_index("yh"), lax.axis_index("yl")
    rows, width = panels[0].shape[1], pair.shape[1]
    cuts = [(at, size) for at, size in CUTS if at < width]

    def load(i, x):
        there = lax.rem(yh * 2 + yl + STEPS[i], 4)
        row = pl.multiple_of(there // 2 * rows, rows)
        slot = pl.multiple_of((x * 2 + lax.rem(there, 2)) * PAIRS, PAIRS)
        source = panels[i].at[x] if i < 3 else panels[3 + x // 2].at[x % 2]
        return pltpu.make_async_copy(source, panel.at[pl.ds(row, rows), pl.ds(slot, PAIRS)], loads.at[i, x])

    def fetch(cut):
        at, size = cuts[cut]
        copies = []
        parts = [(yh, STEPS[i], 0, arrays[0].at[i]) for i in range(4)]
        parts += [(1 - yh, STEPS[i], 0, arrays[i + 1]) for i in range(3)]
        parts += [(1 - yh, 2, i * DEPTH, arrays[i + 4]) for i in range(2)]
        for low, step, skip, source in parts:
            count = source.shape[0]
            slot = pl.multiple_of(lax.rem(z + step, 4) * 2 * PAIRS + low * PAIRS + skip, DEPTH)
            target = block.at[pl.ds(slot, count), pl.ds(at, size)]
            sem = fetches.at[cut, len(copies)]
            copies.append(pltpu.make_async_copy(source.at[:, pl.ds(at, size)], target, sem))
        return copies

    def store(cut, b):
        at, size = cuts[cut]
        here = pl.ds(b * rows, rows)
        source = result.at[here, pl.ds(at, size)]
        return pltpu.make_async_copy(source, out.at[here, pl.ds(at_column + at, size)], stores.at[cut, b])

    copies = [load(i, x) for i in range(4) for x in range(4)]
    pieces = [fetch(cut) for cut in range(len(cuts))]
    for copy in copies + [copy for piece in pieces for copy in piece]:
        copy.start()
    for copy in copies:
        copy.wait()
    for cut, (at, size) in enumerate(cuts):
        for copy in pieces[cut]:
            copy.wait()
        for b in range(2):
            here = (pl.ds(b * rows, rows), pl.ds(at, size))
            residual = jnp.dot(panel[here[0], :], block[:, here[1]], preferred_element_type=jnp.float32)
            denominator = energy[here[0]] - pair[:, here[1]]
            inverse = pl.reciprocal(denominator, approx=True)
            inverse = inverse * (2.0 - denominator * inverse)
            result[here] = (residual * inverse).astype(out.dtype)
            store(cut, b).start()
    for cut in range(len(cuts)):
        for b in range(2):
            store(cut, b).wait()


def product(panels, arrays, energy, pair, started=None):
    rows, width = energy.shape[0], pair.shape[1]
    cuts = len(CUTS)
    operands = [*panels, *arrays, energy, pair] + ([] if started is None else [started])
    at_column = 0 if started is None else width
    return pl.pallas_call(
        functools.partial(product_kernel, at_column),
        out_shape=jax.ShapeDtypeStruct((rows, 2 * width), jnp.bfloat16),
        in_specs=[HBM] * (len(panels) + len(arrays)) + [VMEM] * 2 + ([] if started is None else [HBM]),
        out_specs=HBM,
        scratch_shapes=[
            pltpu.VMEM((rows, 8 * PAIRS), jnp.bfloat16),
            pltpu.VMEM((8 * PAIRS, width), jnp.bfloat16),
            pltpu.VMEM((rows, width), jnp.bfloat16),
            pltpu.SemaphoreType.DMA((4, 4)),
            pltpu.SemaphoreType.DMA((cuts, 9)),
            pltpu.SemaphoreType.DMA((cuts, 2)),
        ],
        input_output_aliases={} if started is None else {len(operands) - 1: 0},
        compiler_params=pltpu.CompilerParams(vmem_limit_bytes=48 << 20),
        cost_estimate=HINT,
        name="product",
    )(*operands)


def place_kernel(columns, piece, out, stores):
    c = lax.axis_index("c")
    copies = []
    for s in range(CHIPS):
        for h in range(2):
            at = (s % 8) * 4 * columns + s // 8 * columns + (1 - c if h else c) * 2 * columns
            target = out.at[:, pl.ds(pl.multiple_of(at, DEPTH), columns)]
            source = piece.at[s, :, pl.ds(h * columns, columns)]
            copies.append(pltpu.make_async_copy(source, target, stores.at[s, h]))
    for copy in copies:
        copy.start()
    for copy in copies:
        copy.wait()


def place(piece):
    rows, width = piece.shape[1:]
    return pl.pallas_call(
        functools.partial(place_kernel, width // 2),
        out_shape=jax.ShapeDtypeStruct((rows, CHIPS * width), jnp.bfloat16),
        in_specs=[VMEM],
        out_specs=HBM,
        scratch_shapes=[pltpu.SemaphoreType.DMA((CHIPS, 2))],
        compiler_params=pltpu.CompilerParams(vmem_limit_bytes=16 << 20),
        cost_estimate=HINT,
        name="place",
    )(piece)


def local(amplitudes, integrals, occ_energy, slab_energy, virt_energy):
    yh, c = lax.axis_index("yh"), lax.axis_index("c")
    portion = amplitudes.shape[0] // CHIPS
    columns = integrals.shape[1] // 2
    after = lax.optimization_barrier

    def pick(value, index, axis):
        return lax.dynamic_index_in_dim(value, index, axis, False)

    def part(h):
        return lax.dynamic_slice(integrals, (0, h * columns), (PAIRS, columns))

    def swap(value):
        return shift(value, "c", 1, 2)

    mine, away = part(yh), part(1 - yh)
    up, down = near(mine, "z")
    other = shift(away, "yh", 1, 2)
    rows = amplitudes.reshape(8, 2, portion, -1)
    kept = pick(rows, c, 1).reshape(8 * portion, -1)
    got = swap(pick(rows, 1 - c, 1).reshape(8 * portion, -1))
    both = jnp.where(c == 0, jnp.concatenate([kept, got], 1), jnp.concatenate([got, kept], 1))
    occ = pick(occ_energy.reshape(8, 2, portion), c, 1).reshape(1, -1)
    along = lax.all_gather(both, "x", axis=0)

    other, along, up, down, occ, slab_energy = after((other, along, up, down, occ, slab_energy))
    others = near(other, "z")
    panels = near(along, Y)
    two = far(up, down, "z")
    here = jnp.stack([mine, up, down, jnp.concatenate(two)])
    panels, slab_energy, occ = after((panels, slab_energy, occ))
    occ_other = shift(occ, "yh", 1, 2)
    other2, slab_other = swap(other), swap(slab_energy)
    others = others + far(*others, "z")
    panels = (along,) + panels + far(*panels, Y)
    energy = jnp.where(yh == 0, jnp.concatenate([occ, occ_other]), jnp.concatenate([occ_other, occ]))
    energy = energy.reshape(-1, 1)

    def pair(slab):
        pairs = (slab[:, None] + virt_energy[None, :]).reshape(2, columns)
        return pick(pairs, yh, 0).reshape(1, -1)

    pairs, pairs2 = pair(slab_energy), pair(slab_other)
    others, here, panels, energy, pairs, pairs2, other2 = after(
        (others, here, panels, energy, pairs, pairs2, other2)
    )
    there = (swap(here), other2) + tuple(swap(value) for value in others)
    update = product(panels, (here, other) + others, energy, pairs)
    update = product(panels, there, energy, pairs2, update)
    return place(lax.all_to_all(update.reshape(CHIPS, portion, -1), PLANE, 0, 0, tiled=True))


def solution(mesh):
    fine = Mesh(mesh.devices.reshape(SIZES), AXES)
    split = P(("z", "yh"), ("x", "yl", "c"))
    return jax.shard_map(
        local,
        mesh=fine,
        in_specs=(split, split, P(("z", "yh")), P(("x", "yl", "c")), P()),
        out_specs=P(AXES, None),
        check_vma=False,
    )
```

```python
import functools

import jax
import jax.numpy as jnp
from jax import lax
from jax.experimental import pallas as pl
from jax.experimental.pallas import tpu as pltpu
from jax.sharding import Mesh, PartitionSpec as P

AXES = ("z", "yh", "x", "yl", "c")
SIZES = (4, 2, 4, 2, 2)
PLANE = ("yh", "x", "yl")
CHIPS = 16
PAIRS = 256
DEPTH = 128
CUTS = ((0, 896), (896, 1024))
STEPS = (0, 1, 3, 2)
Y = ("yh", "yl")
HBM = pl.BlockSpec(memory_space=pltpu.HBM)
VMEM = pl.BlockSpec(memory_space=pltpu.VMEM)
HINT = pl.CostEstimate(flops=10**6, bytes_accessed=1 << 16, transcendentals=0)


def shift(value, axis, step, size):
    return lax.ppermute(value, axis, [((i + step) % size, i) for i in range(size)])


def near(value, axis):
    return shift(value, axis, 1, 4), shift(value, axis, 3, 4)


def far(up, down, axis):
    cut = up.shape[0] // 2
    return shift(up[:cut], axis, 1, 4), shift(down[cut:], axis, 3, 4)


def product_kernel(at_column, *refs):
    panels, arrays, energy, pair = refs[:5], refs[5:11], refs[11], refs[12]
    out, panel, block, result, loads, fetches, stores = refs[-7:]
    z, yh, yl = lax.axis_index("z"), lax.axis_index("yh"), lax.axis_index("yl")
    rows, width = panels[0].shape[1], pair.shape[1]
    cuts = [(at, size) for at, size in CUTS if at < width]

    def load(i, x):
        there = lax.rem(yh * 2 + yl + STEPS[i], 4)
        row = pl.multiple_of(there // 2 * rows, rows)
        slot = pl.multiple_of((x * 2 + lax.rem(there, 2)) * PAIRS, PAIRS)
        source = panels[i].at[x] if i < 3 else panels[3 + x // 2].at[x % 2]
        return pltpu.make_async_copy(source, panel.at[pl.ds(row, rows), pl.ds(slot, PAIRS)], loads.at[i, x])

    def fetch(cut):
        at, size = cuts[cut]
        copies = []
        parts = [(yh, STEPS[i], 0, arrays[0].at[i]) for i in range(4)]
        parts += [(1 - yh, STEPS[i], 0, arrays[i + 1]) for i in range(3)]
        parts += [(1 - yh, 2, i * DEPTH, arrays[i + 4]) for i in range(2)]
        for low, step, skip, source in parts:
            count = source.shape[0]
            slot = pl.multiple_of(lax.rem(z + step, 4) * 2 * PAIRS + low * PAIRS + skip, DEPTH)
            target = block.at[pl.ds(slot, count), pl.ds(at, size)]
            sem = fetches.at[cut, len(copies)]
            copies.append(pltpu.make_async_copy(source.at[:, pl.ds(at, size)], target, sem))
        return copies

    def store(cut, b):
        at, size = cuts[cut]
        here = pl.ds(b * rows, rows)
        source = result.at[here, pl.ds(at, size)]
        return pltpu.make_async_copy(source, out.at[here, pl.ds(at_column + at, size)], stores.at[cut, b])

    copies = [load(i, x) for i in range(4) for x in range(4)]
    pieces = [fetch(cut) for cut in range(len(cuts))]
    for copy in copies + [copy for piece in pieces for copy in piece]:
        copy.start()
    for copy in copies:
        copy.wait()
    for cut, (at, size) in enumerate(cuts):
        for copy in pieces[cut]:
            copy.wait()
        for b in range(2):
            here = (pl.ds(b * rows, rows), pl.ds(at, size))
            residual = jnp.dot(panel[here[0], :], block[:, here[1]], preferred_element_type=jnp.float32)
            denominator = energy[here[0]] - pair[:, here[1]]
            inverse = pl.reciprocal(denominator, approx=True)
            inverse = inverse * (2.0 - denominator * inverse)
            result[here] = (residual * inverse).astype(out.dtype)
            store(cut, b).start()
    for cut in range(len(cuts)):
        for b in range(2):
            store(cut, b).wait()


def product(panels, arrays, energy, pair, started=None):
    rows, width = energy.shape[0], pair.shape[1]
    cuts = len(CUTS)
    operands = [*panels, *arrays, energy, pair] + ([] if started is None else [started])
    at_column = 0 if started is None else width
    return pl.pallas_call(
        functools.partial(product_kernel, at_column),
        out_shape=jax.ShapeDtypeStruct((rows, 2 * width), jnp.bfloat16),
        in_specs=[HBM] * (len(panels) + len(arrays)) + [VMEM] * 2 + ([] if started is None else [HBM]),
        out_specs=HBM,
        scratch_shapes=[
            pltpu.VMEM((rows, 8 * PAIRS), jnp.bfloat16),
            pltpu.VMEM((8 * PAIRS, width), jnp.bfloat16),
            pltpu.VMEM((rows, width), jnp.bfloat16),
            pltpu.SemaphoreType.DMA((4, 4)),
            pltpu.SemaphoreType.DMA((cuts, 9)),
            pltpu.SemaphoreType.DMA((cuts, 2)),
        ],
        input_output_aliases={} if started is None else {len(operands) - 1: 0},
        compiler_params=pltpu.CompilerParams(vmem_limit_bytes=48 << 20),
        cost_estimate=HINT,
        name="product",
    )(*operands)


def place_kernel(columns, piece, out, stores):
    c = lax.axis_index("c")
    copies = []
    for s in range(CHIPS):
        for h in range(2):
            at = (s % 8) * 4 * columns + s // 8 * columns + (1 - c if h else c) * 2 * columns
            target = out.at[:, pl.ds(pl.multiple_of(at, DEPTH), columns)]
            source = piece.at[s, :, pl.ds(h * columns, columns)]
            copies.append(pltpu.make_async_copy(source, target, stores.at[s, h]))
    for copy in copies:
        copy.start()
    for copy in copies:
        copy.wait()


def place(piece):
    rows, width = piece.shape[1:]
    return pl.pallas_call(
        functools.partial(place_kernel, width // 2),
        out_shape=jax.ShapeDtypeStruct((rows, CHIPS * width), jnp.bfloat16),
        in_specs=[VMEM],
        out_specs=HBM,
        scratch_shapes=[pltpu.SemaphoreType.DMA((CHIPS, 2))],
        compiler_params=pltpu.CompilerParams(vmem_limit_bytes=16 << 20),
        cost_estimate=HINT,
        name="place",
    )(piece)


def local(amplitudes, integrals, occ_energy, slab_energy, virt_energy):
    yh, c = lax.axis_index("yh"), lax.axis_index("c")
    portion = amplitudes.shape[0] // CHIPS
    columns = integrals.shape[1] // 2
    after = lax.optimization_barrier

    def pick(value, index, axis):
        return lax.dynamic_index_in_dim(value, index, axis, False)

    def part(h):
        return lax.dynamic_slice(integrals, (0, h * columns), (PAIRS, columns))

    def swap(value):
        return shift(value, "c", 1, 2)

    mine, away = part(yh), part(1 - yh)
    up, down = near(mine, "z")
    other = shift(away, "yh", 1, 2)
    rows = amplitudes.reshape(8, 2, portion, -1)
    kept = pick(rows, c, 1).reshape(8 * portion, -1)
    got = swap(pick(rows, 1 - c, 1).reshape(8 * portion, -1))
    both = jnp.where(c == 0, jnp.concatenate([kept, got], 1), jnp.concatenate([got, kept], 1))
    occ = pick(occ_energy.reshape(8, 2, portion), c, 1).reshape(1, -1)
    along = lax.all_gather(both, "x", axis=0)

    other, along, up, down, occ, slab_energy = after((other, along, up, down, occ, slab_energy))
    others = near(other, "z")
    panels = near(along, Y)
    two = far(up, down, "z")
    here = jnp.stack([mine, up, down, jnp.concatenate(two)])
    panels, slab_energy, occ = after((panels, slab_energy, occ))
    occ_other = shift(occ, "yh", 1, 2)
    other2, slab_other = swap(other), swap(slab_energy)
    others = others + far(*others, "z")
    panels = (along,) + panels + far(*panels, Y)
    energy = jnp.where(yh == 0, jnp.concatenate([occ, occ_other]), jnp.concatenate([occ_other, occ]))
    energy = energy.reshape(-1, 1)

    def pair(slab):
        pairs = (slab[:, None] + virt_energy[None, :]).reshape(2, columns)
        return pick(pairs, yh, 0).reshape(1, -1)

    pairs, pairs2 = pair(slab_energy), pair(slab_other)
    others, here, panels, energy, pairs, pairs2, other2 = after(
        (others, here, panels, energy, pairs, pairs2, other2)
    )
    there = (swap(here), other2) + tuple(swap(value) for value in others)
    update = product(panels, (here, other) + others, energy, pairs)
    update = product(panels, there, energy, pairs2, update)
    return place(lax.all_to_all(update.reshape(CHIPS, portion, -1), PLANE, 0, 0, tiled=True))


def solution(mesh):
    fine = Mesh(mesh.devices.reshape(SIZES), AXES)
    split = P(("z", "yh"), ("x", "yl", "c"))
    return jax.shard_map(
        local,
        mesh=fine,
        in_specs=(split, split, P(("z", "yh")), P(("x", "yl", "c")), P()),
        out_specs=P(AXES, None),
        check_vma=False,
    )
```
